32 devices in a mesh: row: 4 (over y, x), col: 8 (over z, core).
Axes of the slice: x: 2, y: 2, z: 4, core: 2. Of those that a mesh axis runs over, the one named last changes fastest.
Arguments:
- points: float32 [8, 32768], P(None, ('row', 'col')), may hold values from -4 to 4
- point_order: int32 [32, 1024], P(('row', 'col')), may hold values from 0 to 1023, each once within a row
- noise_var: float32 [32768], P(('row', 'col')), may hold values from 0.1 to 3
- inv_scale: float32 [8], replicated, may hold values from 0.2 to 0.6
- basis_vectors: float32 [16, 64, 32768], P(None, None, ('row', 'col')), may hold values from -4 to 4
- current: float32 [64, 32768], P(None, ('row', 'col')), may hold values from -22 to 22
- tile_rows: int32 [4, 8, 64], P('row', 'col'), may hold values from 0 to 31, as said below
- tile_cols: int32 [4, 8, 64], P('row', 'col'), may hold values from 0 to 15
Outputs:
- lanczos_next: float32 [64, 32768], P(None, ('row', 'col'))
- coefficients: float32 [4, 64], replicated
- gradient_product: float32 [64, 32768], P(None, ('row', 'col'))
The draws below stay inside these ranges and needn't reach their ends.
Inputs may be any that keep to these rules, and one draw needn't show every extreme that they name: In each grid cell the 64 pairs (tile_rows, tile_cols) are distinct; each cell lists its 4 pairs with I = J; over all cells no unordered pair of distinct blocks is listed twice: it is listed as (I, J) with I < J when I + J is odd and with I > J when I + J is even.
All inputs are finite; a program needn't handle non-finite values.
Results may differ from the reference program's by a relative error of at most 0.00019.
Values sent between devices are 32-bit elements; how exact they have to be, the bound alone decides.
A program may use at most 128 MiB of HBM per device.

```python
import math
import jax
import jax.numpy as jnp
from jax import lax

FEAT = 8
BLOCK = 256
PROBES = 64
HISTORY = 16
ITERS = 2
PTS_DEV = 1024
BLOCKS_DEV = 4
TILES = 64
SPANS = 32
POINTS = 32768
ROW_BLOCKS = 32
COL_BLOCKS = 16
N_ROW = 4
N_COL = 8


def window_vectors(key):
    shared = jax.random.fold_in(key, 41)
    ramp_up = 1.0 + 2.0 * jnp.arange(POINTS, dtype=jnp.float32) / POINTS
    stored = jnp.clip(jax.random.normal(jax.random.fold_in(shared, 4), (HISTORY, PROBES, POINTS), jnp.float32), -4.0, 4.0)
    fresh_part = jnp.clip(jax.random.normal(jax.random.fold_in(shared, 5), (PROBES, POINTS), jnp.float32), -4.0, 4.0)
    mixture = (fresh_part + 0.4 * stored[HISTORY - 1] + 0.4 * stored[HISTORY - 2]) * ramp_up
    return (stored, mixture)


def draw_basis_vectors(key, part):
    return window_vectors(key)[0]


def draw_current(key, part):
    return window_vectors(key)[1]


def tile_pattern(key):
    pattern_key = jax.random.fold_in(key, 5)
    slot_count = ROW_BLOCKS * COL_BLOCKS
    slot_ids = jnp.arange(slot_count, dtype=jnp.int32)
    local_row = slot_ids // COL_BLOCKS
    local_col = slot_ids % COL_BLOCKS
    row_index = jnp.arange(N_ROW, dtype=jnp.int32)[:, None, None]
    col_index = jnp.arange(N_COL, dtype=jnp.int32)[None, :, None]
    global_row = row_index * ROW_BLOCKS + local_row[None, None, :]
    global_col = (local_col[None, None, :] // BLOCKS_DEV * N_COL + col_index) * BLOCKS_DEV + local_col[None, None, :] % BLOCKS_DEV
    odd_sum = (global_row + global_col) % 2 == 1
    diagonal = global_row == global_col
    stored = diagonal | ((global_row < global_col) == odd_sum)
    open_slot = stored & jnp.logical_not(diagonal)
    random_part = jax.random.randint(pattern_key, (N_ROW, N_COL, slot_count), 0, 4096, jnp.int32)
    base_rank = random_part * slot_count + slot_ids
    boosted = jnp.zeros(base_rank.shape, jnp.bool_)
    for line_mask in (local_row == 0, local_row == ROW_BLOCKS - 1, local_col == 0, local_col == COL_BLOCKS - 1):
        masked = jnp.where(line_mask[None, None, :] & open_slot, base_rank, -1 - slot_ids)
        best_slot = lax.top_k(masked, 1)[1]
        reached = jnp.take_along_axis(masked, best_slot, axis=2) >= 0
        boosted = boosted | (slot_ids == best_slot) & reached
    tier_level = jnp.where(diagonal, 3, jnp.where(boosted, 2, jnp.where(stored, 1, 0)))
    priority = tier_level * (4096 * slot_count) + base_rank
    chosen = lax.top_k(priority, TILES)[1]
    return ((chosen // COL_BLOCKS).astype(jnp.int32), (chosen % COL_BLOCKS).astype(jnp.int32))


def draw_tile_rows(key, part):
    return tile_pattern(key)[0]


def draw_tile_cols(key, part):
    return tile_pattern(key)[1]


def block_levels(own_key, dims, pieces, least, top_value):
    def one(axis_at, shards_of):
        draws = jax.random.uniform(jax.random.fold_in(jax.random.fold_in(own_key, 6), axis_at), (shards_of,), jnp.float32, least / len(pieces), top_value / len(pieces))
        return jnp.repeat(jnp.exp(draws), dims[axis_at] // shards_of).reshape((-1,) + (1,) * (len(dims) - axis_at - 1))

    loudness = one(*pieces[0])
    for cut in pieces[1:]:
        loudness = loudness * one(*cut)
    return loudness


def noise(own_key, shape, width, limit, pieces=(), kind=jnp.bfloat16):
    factor_of = block_levels(own_key, shape, pieces, -0.22, 0.18) if pieces else 1.0
    result = jax.random.normal(own_key, shape, jnp.float32) * width * factor_of
    return jnp.minimum(jnp.maximum(result, -limit), limit).astype(kind)


def setup_inputs(seed: int = 0) -> dict:
    seeds = jax.random.split(jax.random.key(seed), 9)
    points = noise(seeds[0], (FEAT, POINTS), 1.0, 4.0, ((1, 32),), jnp.float32)
    point_order = jax.vmap(lambda own: jax.random.permutation(own, PTS_DEV))(jax.random.split(seeds[1], SPANS)).reshape((SPANS, PTS_DEV)).astype(jnp.int32)
    noise_var = jnp.clip(jnp.exp(math.log(3.0) - 3.4011974 * jax.random.uniform(seeds[2], (POINTS,), jnp.float32) ** block_levels(seeds[2], (POINTS,), ((0, 32),), -0.2, 0.2)), 0.1, 3.0)
    inv_scale = jnp.clip(jnp.exp(jax.random.uniform(seeds[3], (FEAT,), jnp.float32, math.log(0.2), math.log(0.6))), 0.2, 0.6)
    basis_vectors = draw_basis_vectors(jax.random.fold_in(seeds[8], 71), 0)
    current = draw_current(jax.random.fold_in(seeds[8], 71), 0)
    tile_rows = draw_tile_rows(jax.random.fold_in(seeds[8], 71), 0)
    tile_cols = draw_tile_cols(jax.random.fold_in(seeds[8], 71), 0)
    return dict(points=points, point_order=point_order, noise_var=noise_var, inv_scale=inv_scale, basis_vectors=basis_vectors, current=current, tile_rows=tile_rows, tile_cols=tile_cols)


ROOT_THREE = math.sqrt(3.0)
SUPPORT = 3.0
EPSILON = 1e-06
HIGHEST = lax.Precision.HIGHEST

def kernel_tiles(row_points, col_points):
    dist_sq = jnp.zeros((row_points.shape[1], row_points.shape[2], col_points.shape[2]), jnp.float32)
    for feature in range(row_points.shape[0]):
        differ = row_points[feature][:, :, None] - col_points[feature][:, None, :]
        dist_sq = dist_sq + differ * differ
    shifted = dist_sq + EPSILON
    radius = jnp.sqrt(shifted)
    decaying = jnp.exp(-ROOT_THREE * radius)
    matern_part = (1.0 + ROOT_THREE * radius) * decaying
    tapered = jnp.maximum(1.0 - radius / SUPPORT, 0.0)
    taper_cube = tapered * tapered * tapered
    weight = taper_cube * tapered * (1.0 + 4.0 * radius / SUPPORT)
    kernel_tile = matern_part * weight
    slope_tile = shifted * (3.0 * decaying * weight + 20.0 * matern_part * taper_cube / (SUPPORT * SUPPORT))
    return (kernel_tile, slope_tile)

def operate(values, block_points, row_list, col_list, mirror_list, with_slope):
    probe_count = values.shape[0]
    blocked = values.reshape(probe_count, -1, BLOCK)
    layers = 2 if with_slope else 1
    group_size = math.gcd(row_list.shape[0], 8)
    grouped = (row_list.reshape(-1, group_size), col_list.reshape(-1, group_size), mirror_list.reshape(-1, group_size))

    def one_group(totals, listed):
        row_pick, col_pick, mirror_pick = listed
        kernel_tile, slope_tile = kernel_tiles(jnp.take(block_points, row_pick, axis=1), jnp.take(block_points, col_pick, axis=1))
        if with_slope:
            stacked = jnp.stack([kernel_tile, slope_tile])
        else:
            stacked = kernel_tile[None]
        col_side = jnp.take(blocked, col_pick, axis=1)
        row_side = jnp.take(blocked, row_pick, axis=1) * mirror_pick[None, :, None]
        direct = jnp.einsum('pgj,kgij->kpgi', col_side, stacked, precision=HIGHEST)
        mirrored = jnp.einsum('pgi,kgij->kpgj', row_side, stacked, precision=HIGHEST)
        totals = totals.at[:, :, row_pick].add(direct)
        totals = totals.at[:, :, col_pick].add(mirrored)
        return (totals, None)
    totals = jnp.zeros((layers, probe_count, blocked.shape[1], BLOCK), jnp.float32)
    totals, unused = lax.scan(one_group, totals, grouped)
    return totals.reshape(layers, probe_count, -1)

def reference(points, point_order, noise_var, inv_scale, basis_vectors, current, tile_rows, tile_cols):
    offsets = (jnp.arange(SPANS, dtype=jnp.int32) * PTS_DEV)[:, None]
    arrangement = (point_order + offsets).reshape(-1).astype(jnp.int32)
    scaled = jnp.take(points, arrangement, axis=1) * inv_scale[:, None]
    noise_arranged = jnp.take(noise_var, arrangement)
    block_points = scaled.reshape(FEAT, -1, BLOCK)
    row_index = jnp.arange(N_ROW, dtype=jnp.int32)[:, None, None]
    col_index = jnp.arange(N_COL, dtype=jnp.int32)[None, :, None]
    global_row = (row_index * ROW_BLOCKS + tile_rows).reshape(-1).astype(jnp.int32)
    global_col = ((tile_cols // BLOCKS_DEV * N_COL + col_index) * BLOCKS_DEV + tile_cols % BLOCKS_DEV).reshape(-1).astype(jnp.int32)
    mirror_list = (global_row != global_col).astype(jnp.float32)
    earlier = basis_vectors
    coefficient_rows = []
    gradient_product = current
    for iteration in range(ITERS):
        images = operate(current, block_points, global_row, global_col, mirror_list, iteration == 0)
        if iteration == 0:
            gradient_product = images[1]
        image_vec = images[0] + noise_arranged * current
        earlier_dots = jnp.einsum('hpn,pn->hp', earlier, image_vec, precision=HIGHEST) / POINTS
        alpha_now = lax.optimization_barrier(jnp.sum(current * image_vec, axis=1)) / POINTS
        residual_vec = image_vec - alpha_now[:, None] * current - jnp.einsum('hp,hpn->pn', earlier_dots, earlier, precision=HIGHEST)
        beta_now = jnp.sqrt(lax.optimization_barrier(jnp.sum(residual_vec * residual_vec, axis=1)) / POINTS + EPSILON)
        coefficient_rows += [alpha_now, beta_now]
        if iteration + 1 < ITERS:
            earlier = jnp.concatenate([earlier, current[None]], axis=0)
        current = residual_vec / beta_now[:, None]
    return (current, jnp.stack(coefficient_rows), gradient_product)
```

```python
import functools
import math

import jax
import jax.numpy as jnp
from jax import lax
from jax.experimental import pallas as pl
from jax.experimental.pallas import tpu as pltpu
from jax.sharding import PartitionSpec as P

BLOCK = 256
ITERS = 2
GROUP = 2

ROOT_THREE = math.sqrt(3.0)
SUPPORT = 3.0
EPSILON = 1e-06
HIGHEST = lax.Precision.HIGHEST
VMEM_LIMIT = 56 * 1024 * 1024


def split(x):
    high = x.astype(jnp.bfloat16)
    low = (x - high.astype(jnp.float32)).astype(jnp.bfloat16)
    return high, low


def mm(a, b):
    return jnp.dot(a, b, preferred_element_type=jnp.float32)


def load_values(col_values, row_values, col_t, row_v):
    devs, probes, width = col_values.shape
    per = width // BLOCK
    for dev in range(devs):
        for b in range(per):
            block = jnp.transpose(col_values[dev, :, b * BLOCK : (b + 1) * BLOCK])
            col_t[dev * per + b] = jnp.concatenate(split(block), axis=1)

    def one(dev, carry):
        for b in range(per):
            high, low = split(row_values[dev, :, b * BLOCK : (b + 1) * BLOCK])
            row_v[dev * per + b] = jnp.concatenate([high, low], axis=0)
        return carry

    lax.fori_loop(0, row_values.shape[0], one, 0)
    last = row_v.shape[0] - 1
    row_v[last] = jnp.zeros(row_v.shape[1:], jnp.bfloat16)


def products(tile_ref, at, row_at, col_at, mirror_at, col_t, row_v, row_out, col_out):
    direct = mm(tile_ref[at], col_t[col_at])
    direct = direct[:BLOCK] + direct[BLOCK:]
    direct = direct + pltpu.roll(direct, direct.shape[1] // 2, 1)
    lane = lax.broadcasted_iota(jnp.int32, direct.shape, 1)
    half = row_out.shape[1] // BLOCK
    pair = row_at // 2
    row_out[pair // half, pl.ds(pl.multiple_of(pair % half * BLOCK, BLOCK), BLOCK)] += jnp.where(
        lane // (direct.shape[1] // 2) == row_at % 2, direct, 0.0
    )
    left = row_v[mirror_at]
    mirrored = mm(left, tile_ref[at, :BLOCK]) + mm(left, tile_ref[at, BLOCK:])
    devs, probes, width = col_out.shape
    per = width // BLOCK
    col_out[col_at // per, :, pl.ds(pl.multiple_of(col_at % per * BLOCK, BLOCK), BLOCK)] += (
        mirrored[:probes] + mirrored[probes:]
    )


def evaluate(row_points_t, row_at, col_points, col_at, tile_ref, slope_ref, at):
    width = 32
    per = col_points.shape[2] // BLOCK
    feats = col_points.shape[1]
    cols = col_points[col_at // per, :, pl.ds(pl.multiple_of(col_at % per * BLOCK, BLOCK), BLOCK)]
    for chunk in range(BLOCK // width):
        low, top = chunk * width, (chunk + 1) * width
        rows = row_points_t[row_at, low:top, :]
        dist = None
        for f in range(feats):
            differ = rows[:, f : f + 1] - cols[f : f + 1, :]
            dist = differ * differ if dist is None else dist + differ * differ
        shifted = dist + EPSILON
        radius = shifted * lax.rsqrt(shifted)
        decaying = jnp.exp(-ROOT_THREE * radius)
        taper = jnp.maximum(1.0 - radius * (1.0 / SUPPORT), 0.0)
        common = decaying * (taper * taper * taper)
        first = 1.0 + ROOT_THREE * radius
        second = taper * (1.0 + (4.0 / SUPPORT) * radius)
        tile = common * (first * second)
        slope = (shifted * common) * (3.0 * second + (20.0 / (SUPPORT * SUPPORT)) * first)
        high, rest = split(tile)
        tile_ref[at, low:top] = high
        tile_ref[at, BLOCK + low : BLOCK + top] = rest
        high, rest = split(slope)
        slope_ref[at, low:top] = high
        slope_ref[at, BLOCK + low : BLOCK + top] = rest


def first_kernel(
    rows_ref, cols_ref, mirror_ref, col_points, row_points, col_values, row_values,
    tiles, row_k, row_d, col_k, col_d,
    row_points_t, slopes, col_t, row_v,
):
    step = pl.program_id(0)

    @pl.when(step == 0)
    def _():
        load_values(col_values, row_values, col_t, row_v)
        per = row_points.shape[2] // BLOCK

        def one(dev, carry):
            for b in range(per):
                row_points_t[dev * per + b] = jnp.transpose(row_points[dev, :, b * BLOCK : (b + 1) * BLOCK])
            return carry

        lax.fori_loop(0, row_points.shape[0], one, 0)
        for acc in (row_k, row_d, col_k, col_d):
            acc[...] = jnp.zeros_like(acc)

    group = tiles.shape[0]
    for g in range(group):
        t = step * group + g
        evaluate(row_points_t, rows_ref[t], col_points, cols_ref[t], tiles, slopes, g)
        products(tiles, g, rows_ref[t], cols_ref[t], mirror_ref[t], col_t, row_v, row_k, col_k)
        products(slopes, g, rows_ref[t], cols_ref[t], mirror_ref[t], col_t, row_v, row_d, col_d)


def later_kernel(
    rows_ref, cols_ref, mirror_ref, col_values, row_values, tiles,
    row_k, col_k, col_t, row_v,
):
    step = pl.program_id(0)

    @pl.when(step == 0)
    def _():
        load_values(col_values, row_values, col_t, row_v)
        for acc in (row_k, col_k):
            acc[...] = jnp.zeros_like(acc)

    group = tiles.shape[0]
    for g in range(group):
        t = step * group + g
        products(tiles, g, rows_ref[t], cols_ref[t], mirror_ref[t], col_t, row_v, row_k, col_k)


def whole_spec(shape):
    return pl.BlockSpec(shape, lambda *_: (0,) * len(shape))


def tile_products(lists, col_values, row_values, col_points=None, row_points=None, tiles=None):
    count = lists[0].shape[0]
    nr, probes, width = col_values.shape
    nc = row_values.shape[0]
    per = width // BLOCK
    f32, bf16 = jnp.float32, jnp.bfloat16
    row_shape = (nc, width // 2, 2 * probes)
    col_shape = (nr, probes, width)
    tile_shape = (count, 2 * BLOCK, BLOCK)
    group = math.gcd(GROUP, count) if tiles is None else math.gcd(4, count)
    tile_spec = pl.BlockSpec((group, 2 * BLOCK, BLOCK), lambda i, *_: (i, 0, 0))
    values_scratch = [
        pltpu.VMEM((nr * per, BLOCK, 2 * probes), bf16),
        pltpu.VMEM((nc * per + 1, 2 * probes, BLOCK), bf16),
    ]
    params = pltpu.CompilerParams(vmem_limit_bytes=VMEM_LIMIT, dimension_semantics=("arbitrary",))
    flops = 2 * count * 2 * BLOCK * BLOCK * 4 * probes
    if tiles is None:
        operands = (col_points, row_points, col_values, row_values)
        return pl.pallas_call(
            first_kernel,
            grid_spec=pltpu.PrefetchScalarGridSpec(
                num_scalar_prefetch=3,
                grid=(count // group,),
                in_specs=[whole_spec(x.shape) for x in operands],
                out_specs=[tile_spec] + [whole_spec(s) for s in (row_shape, row_shape, col_shape, col_shape)],
                scratch_shapes=[
                    pltpu.VMEM((nc * per, BLOCK, col_points.shape[1]), f32),
                    pltpu.VMEM((group, 2 * BLOCK, BLOCK), bf16),
                    *values_scratch,
                ],
            ),
            out_shape=[jax.ShapeDtypeStruct(tile_shape, bf16)]
            + [jax.ShapeDtypeStruct(s, f32) for s in (row_shape, row_shape, col_shape, col_shape)],
            compiler_params=params,
            cost_estimate=pl.CostEstimate(flops=2 * flops, bytes_accessed=32 << 20, transcendentals=2 * count * BLOCK * BLOCK),
            name="first_tiles",
        )(*lists, *operands)
    return pl.pallas_call(
        later_kernel,
        grid_spec=pltpu.PrefetchScalarGridSpec(
            num_scalar_prefetch=3,
            grid=(count // group,),
            in_specs=[whole_spec(col_values.shape), whole_spec(row_values.shape), tile_spec],
            out_specs=[whole_spec(s) for s in (row_shape, col_shape)],
            scratch_shapes=values_scratch,
        ),
        out_shape=[jax.ShapeDtypeStruct(s, f32) for s in (row_shape, col_shape)],
        compiler_params=params,
        cost_estimate=pl.CostEstimate(flops=flops, bytes_accessed=24 << 20, transcendentals=0),
        name="later_tiles",
    )(*lists, col_values, row_values, tiles)


def reduce_parts(row_part, col_part):
    from_rows = lax.psum_scatter(row_part, "col", scatter_dimension=0, tiled=False)
    from_cols = lax.psum_scatter(col_part, "row", scatter_dimension=0, tiled=False)
    probes, width = from_cols.shape
    pairs = from_rows.reshape(width // (2 * BLOCK), BLOCK, 2, probes)
    return from_cols + jnp.transpose(pairs, (3, 0, 2, 1)).reshape(probes, width)


def on_device(
    points, point_order, noise_var, inv_scale, basis_vectors, current, tile_rows, tile_cols
):
    feature_count = points.shape[0]
    per_device = points.shape[1]
    block_count = per_device // BLOCK
    row_count = lax.axis_size("row")
    col_count = lax.axis_size("col")
    point_total = per_device * row_count * col_count
    arrangement = point_order[0]
    scaled = jnp.take(points, arrangement, axis=1) * inv_scale[:, None]
    noise_here = jnp.take(noise_var, arrangement)
    row_blocks = tile_rows[0, 0]
    col_blocks = tile_cols[0, 0]
    global_row = lax.axis_index("row") * col_count * block_count + row_blocks
    global_col = (
        col_blocks // block_count * col_count + lax.axis_index("col")
    ) * block_count + col_blocks % block_count
    mirror_rows = jnp.where(global_row != global_col, row_blocks, col_count * block_count)
    lists = (row_blocks, col_blocks, mirror_rows)
    earlier = basis_vectors
    coefficient_rows = []
    for iteration in range(ITERS):
        if iteration == 0:
            stacked = jnp.concatenate([scaled, current], axis=0)
            col_side = lax.all_gather(stacked, "row", axis=0)
            row_side = lax.all_gather(stacked, "col", axis=0)
            tiles, row_k, row_d, col_k, col_d = tile_products(
                lists, col_side[:, feature_count:], row_side[:, feature_count:],
                col_side[:, :feature_count], row_side[:, :feature_count],
            )
            gradient_product = reduce_parts(row_d, col_d)
        else:
            col_side = lax.all_gather(current, "row", axis=0)
            row_side = lax.all_gather(current, "col", axis=0)
            row_k, col_k = tile_products(lists, col_side, row_side, tiles=tiles)
        image_vec = reduce_parts(row_k, col_k) + noise_here * current
        earlier_dots, alpha_now = lax.psum(
            (
                jnp.sum(earlier * image_vec[None], axis=2),
                jnp.sum(current * image_vec, axis=1),
            ),
            ("row", "col"),
        )
        earlier_dots = earlier_dots / point_total
        alpha_now = alpha_now / point_total
        residual_vec = (
            image_vec
            - alpha_now[:, None] * current
            - jnp.sum(earlier_dots[:, :, None] * earlier, axis=0)
        )
        residual_sq = (
            lax.psum(jnp.sum(residual_vec * residual_vec, axis=1), ("row", "col")) / point_total
        )
        beta_now = jnp.sqrt(residual_sq + EPSILON)
        coefficient_rows += [alpha_now, beta_now]
        if iteration + 1 < ITERS:
            earlier = jnp.concatenate([earlier, current[None]], axis=0)
        current = residual_vec / beta_now[:, None]
    return (current, jnp.stack(coefficient_rows), gradient_product)


def solution(mesh):
    return jax.shard_map(
        on_device,
        mesh=mesh,
        in_specs=(
            P(None, ("row", "col")),
            P(("row", "col"), None),
            P(("row", "col")),
            P(),
            P(None, None, ("row", "col")),
            P(None, ("row", "col")),
            P("row", "col", None),
            P("row", "col", None),
        ),
        out_specs=(P(None, ("row", "col")), P(), P(None, ("row", "col"))),
        check_vma=False,
    )
```

```python
import functools
import math

import jax
import jax.numpy as jnp
from jax import lax
from jax.experimental import pallas as pl
from jax.experimental.pallas import tpu as pltpu
from jax.sharding import PartitionSpec as P

BLOCK = 256
ITERS = 2
GROUP = 2

ROOT_THREE = math.sqrt(3.0)
SUPPORT = 3.0
EPSILON = 1e-06
HIGHEST = lax.Precision.HIGHEST
VMEM_LIMIT = 56 * 1024 * 1024


def split(x):
    high = x.astype(jnp.bfloat16)
    low = (x - high.astype(jnp.float32)).astype(jnp.bfloat16)
    return high, low


def mm(a, b):
    return jnp.dot(a, b, preferred_element_type=jnp.float32)


def load_values(col_values, row_values, col_t, row_v):
    devs, probes, width = col_values.shape
    per = width // BLOCK
    for dev in range(devs):
        for b in range(per):
            block = jnp.transpose(col_values[dev, :, b * BLOCK : (b + 1) * BLOCK])
            col_t[dev * per + b] = jnp.concatenate(split(block), axis=1)

    def one(dev, carry):
        for b in range(per):
            high, low = split(row_values[dev, :, b * BLOCK : (b + 1) * BLOCK])
            row_v[dev * per + b] = jnp.concatenate([high, low], axis=0)
        return carry

    lax.fori_loop(0, row_values.shape[0], one, 0)
    last = row_v.shape[0] - 1
    row_v[last] = jnp.zeros(row_v.shape[1:], jnp.bfloat16)


def products(tile_ref, at, row_at, col_at, mirror_at, col_t, row_v, row_out, col_out):
    direct = mm(tile_ref[at], col_t[col_at])
    direct = direct[:BLOCK] + direct[BLOCK:]
    direct = direct + pltpu.roll(direct, direct.shape[1] // 2, 1)
    lane = lax.broadcasted_iota(jnp.int32, direct.shape, 1)
    half = row_out.shape[1] // BLOCK
    pair = row_at // 2
    row_out[pair // half, pl.ds(pl.multiple_of(pair % half * BLOCK, BLOCK), BLOCK)] += jnp.where(
        lane // (direct.shape[1] // 2) == row_at % 2, direct, 0.0
    )
    left = row_v[mirror_at]
    mirrored = mm(left, tile_ref[at, :BLOCK]) + mm(left, tile_ref[at, BLOCK:])
    devs, probes, width = col_out.shape
    per = width // BLOCK
    col_out[col_at // per, :, pl.ds(pl.multiple_of(col_at % per * BLOCK, BLOCK), BLOCK)] += (
        mirrored[:probes] + mirrored[probes:]
    )


def evaluate(row_points_t, row_at, col_points, col_at, tile_ref, slope_ref, at):
    width = 32
    per = col_points.shape[2] // BLOCK
    feats = col_points.shape[1]
    cols = col_points[col_at // per, :, pl.ds(pl.multiple_of(col_at % per * BLOCK, BLOCK), BLOCK)]
    for chunk in range(BLOCK // width):
        low, top = chunk * width, (chunk + 1) * width
        rows = row_points_t[row_at, low:top, :]
        dist = None
        for f in range(feats):
            differ = rows[:, f : f + 1] - cols[f : f + 1, :]
            dist = differ * differ if dist is None else dist + differ * differ
        shifted = dist + EPSILON
        radius = shifted * lax.rsqrt(shifted)
        decaying = jnp.exp(-ROOT_THREE * radius)
        taper = jnp.maximum(1.0 - radius * (1.0 / SUPPORT), 0.0)
        common = decaying * (taper * taper * taper)
        first = 1.0 + ROOT_THREE * radius
        second = taper * (1.0 + (4.0 / SUPPORT) * radius)
        tile = common * (first * second)
        slope = (shifted * common) * (3.0 * second + (20.0 / (SUPPORT * SUPPORT)) * first)
        high, rest = split(tile)
        tile_ref[at, low:top] = high
        tile_ref[at, BLOCK + low : BLOCK + top] = rest
        high, rest = split(slope)
        slope_ref[at, low:top] = high
        slope_ref[at, BLOCK + low : BLOCK + top] = rest


def first_kernel(
    feats, rows_ref, cols_ref, mirror_ref, col_side, row_side,
    tiles, row_k, row_d, col_k, col_d,
    row_points_t, slopes, col_t, row_v,
):
    step = pl.program_id(0)
    probes = col_side.shape[1] - feats
    col_points, row_points = col_side.at[:, pl.ds(0, feats)], row_side.at[:, pl.ds(0, feats)]
    col_values, row_values = col_side.at[:, pl.ds(feats, probes)], row_side.at[:, pl.ds(feats, probes)]

    @pl.when(step == 0)
    def _():
        load_values(col_values, row_values, col_t, row_v)
        per = row_points.shape[2] // BLOCK

        def one(dev, carry):
            for b in range(per):
                row_points_t[dev * per + b] = jnp.transpose(row_points[dev, :, b * BLOCK : (b + 1) * BLOCK])
            return carry

        lax.fori_loop(0, row_points.shape[0], one, 0)
        for acc in (row_k, row_d, col_k, col_d):
            acc[...] = jnp.zeros_like(acc)

    group = tiles.shape[0]
    for g in range(group):
        t = step * group + g
        evaluate(row_points_t, rows_ref[t], col_points, cols_ref[t], tiles, slopes, g)
        products(tiles, g, rows_ref[t], cols_ref[t], mirror_ref[t], col_t, row_v, row_k, col_k)
        products(slopes, g, rows_ref[t], cols_ref[t], mirror_ref[t], col_t, row_v, row_d, col_d)


def later_kernel(
    rows_ref, cols_ref, mirror_ref, col_values, row_values, tiles,
    row_k, col_k, col_t, row_v,
):
    step = pl.program_id(0)

    @pl.when(step == 0)
    def _():
        load_values(col_values, row_values, col_t, row_v)
        for acc in (row_k, col_k):
            acc[...] = jnp.zeros_like(acc)

    group = tiles.shape[0]
    for g in range(group):
        t = step * group + g
        products(tiles, g, rows_ref[t], cols_ref[t], mirror_ref[t], col_t, row_v, row_k, col_k)


def whole_spec(shape):
    return pl.BlockSpec(shape, lambda *_: (0,) * len(shape))


def tile_products(lists, col_side, row_side, feats, tiles=None):
    count = lists[0].shape[0]
    nr, stacked, width = col_side.shape
    probes = stacked - feats
    nc = row_side.shape[0]
    per = width // BLOCK
    f32, bf16 = jnp.float32, jnp.bfloat16
    row_shape = (nc, width // 2, 2 * probes)
    col_shape = (nr, probes, width)
    tile_shape = (count, 2 * BLOCK, BLOCK)
    group = math.gcd(GROUP, count) if tiles is None else math.gcd(4, count)
    tile_spec = pl.BlockSpec((group, 2 * BLOCK, BLOCK), lambda i, *_: (i, 0, 0))
    values_scratch = [
        pltpu.VMEM((nr * per, BLOCK, 2 * probes), bf16),
        pltpu.VMEM((nc * per + 1, 2 * probes, BLOCK), bf16),
    ]
    params = pltpu.CompilerParams(vmem_limit_bytes=VMEM_LIMIT, dimension_semantics=("arbitrary",))
    flops = 2 * count * 2 * BLOCK * BLOCK * 4 * probes
    if tiles is None:
        operands = (col_side, row_side)
        return pl.pallas_call(
            functools.partial(first_kernel, feats),
            grid_spec=pltpu.PrefetchScalarGridSpec(
                num_scalar_prefetch=3,
                grid=(count // group,),
                in_specs=[whole_spec(x.shape) for x in operands],
                out_specs=[tile_spec] + [whole_spec(s) for s in (row_shape, row_shape, col_shape, col_shape)],
                scratch_shapes=[
                    pltpu.VMEM((nc * per, BLOCK, feats), f32),
                    pltpu.VMEM((group, 2 * BLOCK, BLOCK), bf16),
                    *values_scratch,
                ],
            ),
            out_shape=[jax.ShapeDtypeStruct(tile_shape, bf16)]
            + [jax.ShapeDtypeStruct(s, f32) for s in (row_shape, row_shape, col_shape, col_shape)],
            compiler_params=params,
            cost_estimate=pl.CostEstimate(flops=2 * flops, bytes_accessed=32 << 20, transcendentals=2 * count * BLOCK * BLOCK),
            name="first_tiles",
        )(*lists, *operands)
    return pl.pallas_call(
        later_kernel,
        grid_spec=pltpu.PrefetchScalarGridSpec(
            num_scalar_prefetch=3,
            grid=(count // group,),
            in_specs=[whole_spec(col_side.shape), whole_spec(row_side.shape), tile_spec],
            out_specs=[whole_spec(s) for s in (row_shape, col_shape)],
            scratch_shapes=values_scratch,
        ),
        out_shape=[jax.ShapeDtypeStruct(s, f32) for s in (row_shape, col_shape)],
        compiler_params=params,
        cost_estimate=pl.CostEstimate(flops=flops, bytes_accessed=24 << 20, transcendentals=0),
        name="later_tiles",
    )(*lists, col_side, row_side, tiles)


MESH = pl.DeviceIdType.MESH


def greet(devices):
    barrier = pltpu.get_barrier_semaphore()
    for device in devices:
        pl.semaphore_signal(barrier, inc=1, device_id=device, device_id_type=MESH)
    pl.semaphore_wait(barrier, len(devices))


def gather_kernel(nr, nc, own, col_side, row_side, send_row, recv_row, send_col, recv_col, send_pair, local):
    r, c = lax.axis_index("row"), lax.axis_index("col")
    partner = c + 1 - 2 * lax.rem(c, 2)
    along = [lax.rem(c + 2 * k, nc) for k in range(1, nc // 2)]
    across = [lax.rem(r + k, nr) for k in range(1, nr)]
    greet([(r, partner)] + [(r, to) for to in along] + [(to, c) for to in across])

    def to_row(src, slot, sem, to):
        return pltpu.make_async_remote_copy(
            src_ref=src, dst_ref=row_side.at[slot], send_sem=sem, recv_sem=recv_row.at[slot],
            device_id=(r, to), device_id_type=MESH,
        )

    def to_col(k, slot, to):
        return pltpu.make_async_remote_copy(
            src_ref=own, dst_ref=col_side.at[slot], send_sem=send_col.at[k], recv_sem=recv_col.at[slot],
            device_id=(to, c), device_id_type=MESH,
        )

    sent = []
    for k, to in enumerate(along):
        sent.append(to_row(own, c, send_row.at[k], to))
        sent[-1].start()
    for k, to in enumerate(across):
        sent.append(to_col(k, r, to))
        sent[-1].start()
    sent.append(to_row(own, c, send_pair.at[0], partner))
    sent[-1].start()
    here = [
        pltpu.make_async_copy(own, row_side.at[c], local.at[0]),
        pltpu.make_async_copy(own, col_side.at[r], local.at[1]),
    ]
    for copy in here:
        copy.start()
    for k in range(len(along)):
        source = lax.rem(c + nc - 2 * (k + 1), nc)
        to_row(own, source, send_row.at[k], source).wait_recv()
        sent.append(to_row(row_side.at[source], source, send_pair.at[k + 1], partner))
        sent[-1].start()
    for k in range(nc // 2):
        source = lax.rem(partner + nc - 2 * k, nc)
        to_row(own, source, send_pair.at[k], partner).wait_recv()
    for k in range(len(across)):
        source = lax.rem(r + nr - (k + 1), nr)
        to_col(k, source, source).wait_recv()
    for copy in sent:
        copy.wait_send()
    for copy in here:
        copy.wait()


def both_sides(own, ident):
    nr, nc = lax.axis_size("row"), lax.axis_size("col")
    anywhere = pl.BlockSpec(memory_space=pl.ANY)
    dma = pltpu.SemaphoreType.DMA
    return pl.pallas_call(
        functools.partial(gather_kernel, nr, nc),
        out_shape=[jax.ShapeDtypeStruct((n, *own.shape), own.dtype) for n in (nr, nc)],
        in_specs=[pl.BlockSpec(memory_space=pltpu.VMEM)],
        out_specs=[anywhere, anywhere],
        scratch_shapes=[
            dma((nc // 2,)), dma((nc,)), dma((nr,)), dma((nr,)), dma((nc // 2,)), dma((2,)),
        ],
        compiler_params=pltpu.CompilerParams(collective_id=ident, has_side_effects=True),
        name="gather_sides",
    )(own)


def total_kernel(nr, nc, own, out, first, second, send_one, recv_one, send_two, recv_two):
    r, c = lax.axis_index("row"), lax.axis_index("col")
    along = [lax.rem(c + k, nc) for k in range(1, nc)]
    across = [lax.rem(r + k, nr) for k in range(1, nr)]
    greet([(r, to) for to in along] + [(to, c) for to in across])

    def copy_to(slots, slot, send, recv, device):
        return pltpu.make_async_remote_copy(
            src_ref=slots.at[slot], dst_ref=slots.at[slot], send_sem=send, recv_sem=recv.at[slot],
            device_id=device, device_id_type=MESH,
        )

    first[c] = own[...]
    sent = []
    for k, to in enumerate(along):
        sent.append(copy_to(first, c, send_one.at[k], recv_one, (r, to)))
        sent[-1].start()
    for k, to in enumerate(along):
        copy_to(first, to, send_one.at[k], recv_one, (r, to)).wait_recv()
    total = first[0]
    for slot in range(1, nc):
        total = total + first[slot]
    second[r] = total
    for k, to in enumerate(across):
        sent.append(copy_to(second, r, send_two.at[k], recv_two, (to, c)))
        sent[-1].start()
    for k, to in enumerate(across):
        copy_to(second, to, send_two.at[k], recv_two, (to, c)).wait_recv()
    total = second[0]
    for slot in range(1, nr):
        total = total + second[slot]
    out[...] = total
    for copy in sent:
        copy.wait_send()


def sum_all(values, ident):
    nr, nc = lax.axis_size("row"), lax.axis_size("col")
    count, probes = values.shape
    shape = (-(-count // 8) * 8, -(-probes // 128) * 128)
    padded = jnp.pad(values, ((0, shape[0] - count), (0, shape[1] - probes)))
    vmem = pl.BlockSpec(memory_space=pltpu.VMEM)
    dma = pltpu.SemaphoreType.DMA
    summed = pl.pallas_call(
        functools.partial(total_kernel, nr, nc),
        out_shape=jax.ShapeDtypeStruct(shape, jnp.float32),
        in_specs=[vmem],
        out_specs=vmem,
        scratch_shapes=[
            pltpu.VMEM((nc, *shape), jnp.float32), pltpu.VMEM((nr, *shape), jnp.float32),
            dma((nc,)), dma((nc,)), dma((nr,)), dma((nr,)),
        ],
        compiler_params=pltpu.CompilerParams(collective_id=ident, has_side_effects=True),
        name="sum_all",
    )(padded)
    return summed[:count, :probes]


def reduce_parts(row_part, col_part):
    from_rows = lax.psum_scatter(row_part, "col", scatter_dimension=0, tiled=False)
    from_cols = lax.psum_scatter(col_part, "row", scatter_dimension=0, tiled=False)
    probes, width = from_cols.shape
    pairs = from_rows.reshape(width // (2 * BLOCK), BLOCK, 2, probes)
    return from_cols + jnp.transpose(pairs, (3, 0, 2, 1)).reshape(probes, width)


def on_device(
    points, point_order, noise_var, inv_scale, basis_vectors, current, tile_rows, tile_cols
):
    feature_count = points.shape[0]
    per_device = points.shape[1]
    block_count = per_device // BLOCK
    row_count = lax.axis_size("row")
    col_count = lax.axis_size("col")
    point_total = per_device * row_count * col_count
    arrangement = point_order[0]
    scaled = jnp.take(points, arrangement, axis=1) * inv_scale[:, None]
    noise_here = jnp.take(noise_var, arrangement)
    row_blocks = tile_rows[0, 0]
    col_blocks = tile_cols[0, 0]
    global_row = lax.axis_index("row") * col_count * block_count + row_blocks
    global_col = (
        col_blocks // block_count * col_count + lax.axis_index("col")
    ) * block_count + col_blocks % block_count
    mirror_rows = jnp.where(global_row != global_col, row_blocks, col_count * block_count)
    lists = (row_blocks, col_blocks, mirror_rows)
    earlier = basis_vectors
    coefficient_rows = []
    for iteration in range(ITERS):
        if iteration == 0:
            stacked = jnp.concatenate([scaled, current], axis=0)
            col_side, row_side = both_sides(stacked, 0)
            tiles, row_k, row_d, col_k, col_d = tile_products(lists, col_side, row_side, feature_count)
            gradient_product = reduce_parts(row_d, col_d)
        else:
            col_side, row_side = both_sides(current, 1)
            row_k, col_k = tile_products(lists, col_side, row_side, 0, tiles)
        image_vec = reduce_parts(row_k, col_k) + noise_here * current
        partial = jnp.concatenate(
            [jnp.sum(earlier * image_vec[None], axis=2), jnp.sum(current * image_vec, axis=1)[None]]
        )
        dots = sum_all(partial, 2 + 2 * iteration) / point_total
        earlier_dots, alpha_now = dots[:-1], dots[-1]
        residual_vec = (
            image_vec
            - alpha_now[:, None] * current
            - jnp.sum(earlier_dots[:, :, None] * earlier, axis=0)
        )
        residual_sq = (
            sum_all(jnp.sum(residual_vec * residual_vec, axis=1)[None], 3 + 2 * iteration)[0] / point_total
        )
        beta_now = jnp.sqrt(residual_sq + EPSILON)
        coefficient_rows += [alpha_now, beta_now]
        if iteration + 1 < ITERS:
            earlier = jnp.concatenate([earlier, current[None]], axis=0)
        current = residual_vec / beta_now[:, None]
    return (current, jnp.stack(coefficient_rows), gradient_product)


def solution(mesh):
    return jax.shard_map(
        on_device,
        mesh=mesh,
        in_specs=(
            P(None, ("row", "col")),
            P(("row", "col"), None),
            P(("row", "col")),
            P(),
            P(None, None, ("row", "col")),
            P(None, ("row", "col")),
            P("row", "col", None),
            P("row", "col", None),
        ),
        out_specs=(P(None, ("row", "col")), P(), P(None, ("row", "col"))),
        check_vma=False,
    )
```
